32 devices in a mesh: group: 8 (over z, x), mp: 4 (over y, core).
Axes of the slice: x: 2, y: 2, z: 4, core: 2. Of those that a mesh axis runs over, the one named last changes fastest.
Arguments:
- tokens: bfloat16 [8192, 2048], P('group', 'mp'), may hold values from -6 to 6
- in_gain: float32 [2048], replicated, may hold values from 0.5 to 1.5
- trainer_qkv: float32 [2048, 6144], P(('group', 'mp')), may hold values from -0.125 to 0.125
- head_order: int32 [16], replicated, may hold values from 0 to 15, each once
- conv_weight: float32 [4, 6144], P(None, 'mp'), may hold values from -3 to 3
- beta_weight: bfloat16 [2048, 16], P(None, 'mp'), may hold values from -0.125 to 0.125
- beta_bias: float32 [16], P('mp'), may hold values from -4 to 3
- out_gain: float32 [128], replicated, may hold values from 0.5 to 1.5
- lengths: int32 [8, 8], P('group'), may hold values from 1 to 8, 16 in all within a row
- prior_states: float32 [64, 16, 128, 128], P('group', 'mp'), may hold values from -0.6 to 0.6
- page_table: int32 [64], P('group'), may hold values from 0 to 63, as said below
- o_weight: bfloat16 [2048, 2048], P('mp', 'group'), may hold values from -0.1875 to 0.1875
- gate_weight: bfloat16 [2048, 5632], P('group', 'mp'), may hold values from -0.125 to 0.125
- up_weight: bfloat16 [2048, 5632], P('group', 'mp'), may hold values from -0.125 to 0.125
- down_weight: bfloat16 [5632, 2048], P('mp', 'group'), may hold values from -0.109375 to 0.109375
Outputs:
- attended: bfloat16 [8192, 2048], P('group', 'mp')
- state_pages: float32 [64, 16, 128, 128], P('group', 'mp')
- layer_out: bfloat16 [8192, 2048], P('group', 'mp')
The draws below stay inside these ranges and needn't reach their ends.
Inputs may be any that keep to these rules, and one draw needn't show every extreme that they name: lengths count blocks of 64 tokens; the lengths of one group sum to 16; the longest of each group is 8. `page_table`: a permutation of the 64 pages; page p lies on group p // 8; the 8 slots of one group name pages of exactly 4 groups, exactly 2 pages of each.
All inputs are finite; a program needn't handle non-finite values.
Results may differ from the reference program's by a relative error of at most 0.018.
Values may be sent and summed in bfloat16 or wider, within the bound.
A program may use at most 128 MiB of HBM per device.

```python
import math
import jax
import jax.numpy as jnp
import numpy as np
from jax import lax

D = 2048
H = 16
DK = 128
FF = 5632
CONV = 4
SPAN = 64
MOST_CH = 8
NCH = 16
REQ = 8
CAP = 2
TOKG = 1024
GROUPS = 8
TOKENS = 8192
PAGES = 64
N_MP = 4


def shuffle_row(row_key):
    return jax.random.permutation(row_key, REQ)


def draw_page_table(key, part):
    first_key, second_key = jax.random.split(jax.random.fold_in(key, 7))
    spread_ids = jax.random.permutation(first_key, GROUPS).astype(jnp.int32)
    shift_ids = jnp.arange(GROUPS, dtype=jnp.int32)
    priority = jnp.where(shift_ids == 1, 0, jnp.where(shift_ids == GROUPS // 2, 1, jnp.where(shift_ids == GROUPS - 1, 2, 3 + spread_ids))).astype(jnp.int32)
    offsets = jnp.argsort(priority, stable=True).astype(jnp.int32)[:REQ // CAP]
    shuffled = jax.vmap(shuffle_row)(jax.random.split(second_key, GROUPS)).astype(jnp.int32)
    sources = jnp.arange(GROUPS, dtype=jnp.int32)[:, None]
    bundle = shuffled // CAP
    within = shuffled % CAP
    destination = (sources + jnp.take(offsets, bundle).astype(jnp.int32)) % GROUPS
    return (destination * REQ + bundle * CAP + within).reshape(-1).astype(jnp.int32)


def spiked(array, own_key, source, target, shards_of, factor):
    def block_of(axis_at):
        return (jnp.arange(array.shape[axis_at]) // (array.shape[axis_at] // shards_of)).reshape((-1,) + (1,) * (array.ndim - 1 - axis_at))

    first = jax.random.permutation(own_key, shards_of)[block_of(target)]
    second = (block_of(target) + shards_of // 2) % shards_of
    return jnp.where((block_of(source) == first) | (block_of(source) == second), factor * array, array)


def block_scale(stream_key, dims, cuts, least, top_value):
    loudness, own = 1.0, jax.random.fold_in(stream_key, 6)
    for dim, parts in cuts:
        draws = jnp.exp(jax.random.uniform(jax.random.fold_in(own, dim), (parts,), jnp.float32, least / len(cuts), top_value / len(cuts)))
        loudness = loudness * jnp.repeat(draws, dims[dim] // parts).reshape([-1 if axis == dim else 1 for axis in range(len(dims))])
    return loudness


def length_profile(count, total, reach, slope):
    portions = [(1 << 20) // math.isqrt(standing ** slope) + 1 for standing in range(2, count + 1)]
    spare, counts = total - reach - (count - 1), [1] * (count - 1)
    while spare > 0:
        candidates = [i for i in range(count - 1) if counts[i] < reach]
        whole, remaining = sum([portions[i] for i in candidates]), spare
        for i in candidates:
            extra = min(reach - counts[i], max(1, remaining * portions[i] // whole), spare)
            counts[i] = counts[i] + extra
            spare = spare - extra
    return np.array([reach] + counts)


def uneven_parts(own_key, number_of, total, bound, slope):
    if number_of == 2:
        one = jax.random.randint(own_key, (), max(1, total - bound), min(bound, total - 1) + 1)
        return jnp.stack([one, total - one])
    sizes = jnp.asarray(length_profile(number_of, total, bound, slope), jnp.int32)
    pairs = (number_of - 1) // 2
    source_of, sink = sizes[1:1 + 2 * pairs:2], sizes[2:2 + 2 * pairs:2]
    slack = jnp.minimum(source_of - 1, bound - sink)
    moved = jax.random.randint(jax.random.fold_in(own_key, 1), (pairs,), 0, 1 << 20) % (slack + 1)
    sizes = sizes.at[1:1 + 2 * pairs:2].set(source_of - moved).at[2:2 + 2 * pairs:2].set(sink + moved)
    return sizes[jax.random.permutation(jax.random.fold_in(own_key, 2), number_of)]


def centred(key, dims, spread, bound, cuts=(), kind=jnp.bfloat16):
    drawn = jax.random.normal(key, dims, jnp.float32) * spread
    if len(cuts) > 0:
        drawn = block_scale(key, dims, cuts, -0.22, 0.18) * drawn
    return jnp.clip(drawn, min=-bound, max=bound).astype(kind)


def heavy_noise(rng, dims, deviation, most, cuts, heavy, held_as=jnp.bfloat16):
    drawn = deviation * jax.random.normal(rng, dims, jnp.float32)
    if cuts:
        drawn = drawn * block_scale(rng, dims, cuts, -0.22, 0.18)
    return jnp.clip(spiked(drawn, jax.random.fold_in(rng, 3), *heavy), -most, most).astype(held_as)


def setup_inputs(seed: int = 0) -> dict:
    arg_keys = jax.random.split(jax.random.key(seed), 16)
    tokens = centred(arg_keys[0], (TOKENS, D), 1.0, 6.0, ((0, 8), (1, 4)))
    in_gain = jnp.clip(1.0 + 0.1 * jax.random.normal(arg_keys[1], (D,), jnp.float32), 0.5, 1.5)
    trainer_qkv = centred(arg_keys[2], (D, H * 3 * DK), D ** -0.5, 0.125, ((0, 32),), jnp.float32)
    head_order = jax.random.permutation(arg_keys[3], H).astype(jnp.int32)
    conv_weight = centred(arg_keys[4], (CONV, H * 3 * DK), CONV ** -0.5, 3.0, ((1, 4),), jnp.float32)
    beta_weight = centred(arg_keys[5], (D, H), D ** -0.5, 0.125, ((1, 4),))
    beta_bias = jnp.clip(-4.0 + 7.0 * jax.random.uniform(arg_keys[6], (H,), jnp.float32) ** block_scale(arg_keys[6], (H,), ((0, 4),), -0.2, 0.2), -4.0, 3.0)
    out_gain = jnp.clip(1.0 + 0.1 * jax.random.normal(arg_keys[7], (DK,), jnp.float32), 0.5, 1.5)
    lengths = jax.vmap(lambda own: uneven_parts(own, REQ, NCH, MOST_CH, 2))(jax.random.split(arg_keys[8], GROUPS)).reshape((GROUPS, REQ)).astype(jnp.int32)
    prior_states = centred(arg_keys[9], (PAGES, H, DK, DK), 0.1, 0.6, ((0, 8), (1, 4)), jnp.float32)
    page_table = draw_page_table(jax.random.fold_in(arg_keys[15], 71), 0)
    o_weight = heavy_noise(arg_keys[11], (H * DK, D), (H * DK) ** -0.5, 0.1875, ((0, 4), (1, 8)), (0, 1, 8, 2.0))
    gate_weight = centred(arg_keys[12], (D, FF), D ** -0.5, 0.125, ((0, 8), (1, 4)))
    up_weight = centred(arg_keys[13], (D, FF), D ** -0.5, 0.125, ((0, 8), (1, 4)))
    down_weight = heavy_noise(arg_keys[14], (FF, D), FF ** -0.5, 0.109375, ((0, 4), (1, 8)), (0, 1, 8, 2.0))
    return {"tokens": tokens, "in_gain": in_gain, "trainer_qkv": trainer_qkv, "head_order": head_order, "conv_weight": conv_weight, "beta_weight": beta_weight, "beta_bias": beta_bias, "out_gain": out_gain, "lengths": lengths, "prior_states": prior_states, "page_table": page_table, "o_weight": o_weight, "gate_weight": gate_weight, "up_weight": up_weight, "down_weight": down_weight}


EPSILON = 1e-06

def unit_rows(matrix):
    return matrix * lax.rsqrt(lax.optimization_barrier(jnp.sum(matrix * matrix, axis=-1, keepdims=True)) + EPSILON)

def normalize_rows(matrix, scaling):
    widened = matrix.astype(jnp.float32)
    return widened * lax.rsqrt(lax.optimization_barrier(jnp.mean(widened * widened, axis=-1, keepdims=True)) + EPSILON) * scaling

def segment_layout(lengths_row, span_total, span_rows):
    lengths_row = lengths_row.astype(jnp.int32)
    starts = (jnp.cumsum(lengths_row) - lengths_row).astype(jnp.int32)
    span_ids = jnp.arange(span_total, dtype=jnp.int32)
    seg_of_span = (lax.optimization_barrier(jnp.sum((span_ids[:, None] >= starts[None, :]).astype(jnp.int32), axis=1)) - 1).astype(jnp.int32)
    is_start = jnp.any(span_ids[:, None] == starts[None, :], axis=1)
    positions = jnp.arange(span_total * span_rows, dtype=jnp.int32)
    token_seg = jnp.repeat(seg_of_span, span_rows)
    offset = (positions - jnp.take(starts, token_seg) * span_rows).astype(jnp.int32)
    return (starts, seg_of_span, is_start, token_seg, offset)

def convolve(rows_wide, history, weight, offset, token_seg):
    row_total = rows_wide.shape[0]
    tap_count = weight.shape[0]
    extended = jnp.concatenate([history, rows_wide], axis=0)
    summed = jnp.zeros(rows_wide.shape, jnp.float32)
    for lag_index in range(tap_count):
        lagged = extended[tap_count - 1 - lag_index:tap_count - 1 - lag_index + row_total] * weight[lag_index]
        permitted_mask = (offset >= lag_index) | (token_seg == 0)
        summed = summed + jnp.where(permitted_mask[:, None], lagged, 0.0)
    return summed

def prepare(span_block, key_feature_width):
    active = jax.nn.silu(span_block)
    row_total = span_block.shape[0]
    split_rows = active.reshape(row_total, -1, 3, key_feature_width).transpose(1, 2, 0, 3)
    query_matrix = unit_rows(split_rows[:, 0]) * key_feature_width ** (-0.5)
    lookup_entries_by_token = unit_rows(split_rows[:, 1])
    value_rows = split_rows[:, 2]
    return (query_matrix, lookup_entries_by_token, value_rows)

def span_step(carried_summary_memory, query_matrix, lookup_entries_by_token, value_rows, gating):
    numeric_accuracy_mode = lax.Precision.HIGHEST
    row_total = query_matrix.shape[1]
    key_feature_width = lookup_entries_by_token.shape[2]
    strict = jnp.tril(jnp.ones((row_total, row_total), jnp.float32), -1)
    inclusive = jnp.tril(jnp.ones((row_total, row_total), jnp.float32))
    gram = jnp.einsum('hik,hjk->hij', lookup_entries_by_token, lookup_entries_by_token, precision=numeric_accuracy_mode)
    system = jnp.eye(row_total, dtype=jnp.float32) + gating[:, :, None] * gram * strict
    solve_target_vector = jnp.concatenate([lookup_entries_by_token, value_rows], axis=2) * gating[:, :, None]
    solution_matrix = lax.linalg.triangular_solve(system, solve_target_vector, left_side=True, lower=True)
    corrected_content_entries = solution_matrix[:, :, key_feature_width:] - jnp.einsum('xsi,xin->xsn', solution_matrix[:, :, :key_feature_width], carried_summary_memory, precision=numeric_accuracy_mode)
    attention_scores = jnp.einsum('hik,hjk->hij', query_matrix, lookup_entries_by_token, precision=numeric_accuracy_mode) * inclusive
    output_matrix_rows = jnp.einsum('xsi,xin->xsn', query_matrix, carried_summary_memory, precision=numeric_accuracy_mode) + jnp.einsum('pzd,pdu->pzu', attention_scores, corrected_content_entries, precision=numeric_accuracy_mode)
    carried_summary_memory = carried_summary_memory + jnp.einsum('jtc,jtb->jcb', lookup_entries_by_token, corrected_content_entries, precision=numeric_accuracy_mode)
    return (output_matrix_rows, carried_summary_memory)

def span_at(span_index, carried_summary_memory, initial, convolved, gating_all, seg_of_span, is_start, span_rows, key_feature_width):
    span_block = lax.dynamic_slice_in_dim(convolved, span_index * span_rows, span_rows, 0)
    gating = lax.dynamic_slice_in_dim(gating_all, span_index * span_rows, span_rows, 0).T
    opening = initial[seg_of_span[span_index]]
    carried_summary_memory = jnp.where(is_start[span_index], opening, carried_summary_memory)
    query_matrix, lookup_entries_by_token, value_rows = prepare(span_block, key_feature_width)
    return span_step(carried_summary_memory, query_matrix, lookup_entries_by_token, value_rows, gating)

def blockwise_sum(left, right, block_count):
    width = left.shape[1] // block_count
    summed = jnp.zeros((left.shape[0], right.shape[1]), jnp.float32)
    for block_index in range(block_count):
        block_term = jnp.dot(left[:, block_index * width:(block_index + 1) * width].astype(jnp.float32), right[block_index * width:(block_index + 1) * width].astype(jnp.float32), preferred_element_type=jnp.float32).astype(jnp.bfloat16)
        summed = summed + lax.optimization_barrier(block_term).astype(jnp.float32)
    return summed

def reference(tokens, in_gain, trainer_qkv, head_order, conv_weight, beta_weight, beta_bias, out_gain, lengths, prior_states, page_table, o_weight, gate_weight, up_weight, down_weight):
    joined_width = 3 * DK
    slot_of_head = jnp.argsort(head_order).astype(jnp.int32)
    qkv_weight = jnp.take(trainer_qkv.reshape(D, H, joined_width), slot_of_head, axis=1).reshape(D, H * joined_width).astype(jnp.bfloat16)
    handed_memory = jnp.zeros((H, DK, DK), jnp.float32)
    handed_rows = jnp.zeros((CONV - 1, H * joined_width), jnp.float32)
    attended_parts = []
    final_parts = []
    for group_index in range(GROUPS):
        group_tokens = tokens[group_index * TOKG:(group_index + 1) * TOKG]
        normed = normalize_rows(group_tokens, in_gain).astype(jnp.bfloat16)
        projected = jnp.dot(normed.astype(jnp.float32), qkv_weight.astype(jnp.float32), preferred_element_type=jnp.float32).astype(jnp.bfloat16)
        gating_all = jax.nn.sigmoid(jnp.dot(normed.astype(jnp.float32), beta_weight.astype(jnp.float32), preferred_element_type=jnp.float32) + beta_bias)
        starts, seg_of_span, is_start, token_seg, offset = segment_layout(lengths[group_index], NCH, SPAN)
        linked = group_index > 0
        history = jnp.where(linked, handed_rows, 0.0)
        convolved = convolve(projected.astype(jnp.float32), history, conv_weight, offset, token_seg)
        initial = prior_states[group_index * REQ:(group_index + 1) * REQ]
        initial = initial.at[0].set(jnp.where(linked, handed_memory, initial[0]))

        def advance(carried_summary_memory, span_index):
            output_matrix_rows, carried_summary_memory = span_at(span_index, carried_summary_memory, initial, convolved, gating_all, seg_of_span, is_start, SPAN, DK)
            return (carried_summary_memory, (output_matrix_rows, carried_summary_memory))
        last_memory, (outputs, memories) = lax.scan(advance, jnp.zeros((H, DK, DK), jnp.float32), jnp.arange(NCH, dtype=jnp.int32))
        last_spans = (starts + lengths[group_index].astype(jnp.int32) - 1).astype(jnp.int32)
        final_parts.append(jnp.take(memories, last_spans, axis=0))
        handed_memory = last_memory
        handed_rows = projected[TOKG - (CONV - 1):].astype(jnp.float32)
        mixed = outputs.transpose(0, 2, 1, 3).reshape(TOKG, H, DK)
        attended_parts.append(normalize_rows(mixed, out_gain).astype(jnp.bfloat16).reshape(TOKG, H * DK))
    attended = jnp.concatenate(attended_parts, axis=0)
    finals = jnp.concatenate(final_parts, axis=0)
    state_pages = jnp.zeros_like(finals).at[page_table].set(finals)
    mixer_sum = blockwise_sum(attended, o_weight, N_MP)
    residual_one = (tokens.astype(jnp.float32) + mixer_sum).astype(jnp.bfloat16)
    post_normed = normalize_rows(residual_one, 1.0).astype(jnp.bfloat16)
    gate_sums = jnp.dot(post_normed.astype(jnp.float32), gate_weight.astype(jnp.float32), preferred_element_type=jnp.float32)
    up_sums = jnp.dot(post_normed.astype(jnp.float32), up_weight.astype(jnp.float32), preferred_element_type=jnp.float32)
    hidden = (jax.nn.silu(gate_sums) * up_sums).astype(jnp.bfloat16)
    feed_sum = blockwise_sum(hidden, down_weight, N_MP)
    layer_out = (residual_one.astype(jnp.float32) + feed_sum).astype(jnp.bfloat16)
    return (attended, state_pages, layer_out)
```

```python
from functools import partial

import jax
import jax.numpy as jnp
from jax import lax
from jax.experimental import pallas as pl
from jax.experimental.pallas import tpu as pltpu
from jax.sharding import PartitionSpec as P

SPAN = 64
EPSILON = 1e-06
F32 = jnp.float32
BF16 = jnp.bfloat16
MIB = 1 << 20


def from_behind(value, axis, steps):
    count = lax.axis_size(axis)
    initial, last = (max(0, -steps), min(count, count - steps))
    return lax.ppermute(value, axis, [(source, source + steps) for source in range(initial, last)])


def normalize_rows(matrix, scaling):
    widened = matrix.astype(F32)
    return (
        widened * lax.rsqrt(jnp.mean(widened * widened, axis=-1, keepdims=True) + EPSILON) * scaling
    )


def mm(a, b):
    return lax.dot_general(a, b, (((1,), (0,)), ((), ())), preferred_element_type=F32)


def mm_nt(a, b):
    return lax.dot_general(a, b, (((1,), (1,)), ((), ())), preferred_element_type=F32)


def mm_tn(a, b):
    return lax.dot_general(a, b, (((0,), (0,)), ((), ())), preferred_element_type=F32)


def two(x):
    high = x.astype(BF16)
    return high, (x - high.astype(F32)).astype(BF16)


def mm3(a, b, product=mm):
    return product(a[0], b[0]) + (product(a[0], b[1]) + product(a[1], b[0]))


def order_kernel(slot_ref, x_ref, o_ref):
    o_ref[0] = x_ref[...].astype(BF16)


def order_heads(trainer, slot_of_head, parts, heads, joined):
    rows = trainer.shape[0]
    per = heads // parts
    return pl.pallas_call(
        order_kernel,
        grid_spec=pltpu.PrefetchScalarGridSpec(
            num_scalar_prefetch=1,
            grid=(heads,),
            in_specs=[pl.BlockSpec((rows, joined), lambda h, s: (0, s[h]))],
            out_specs=pl.BlockSpec((1, rows, joined), lambda h, s: (h // per, 0, h % per)),
        ),
        out_shape=jax.ShapeDtypeStruct((parts, rows, per * joined), BF16),
        name="order_heads",
    )(slot_of_head, trainer)


def intra_one(flag, before, rows, taps, gating, heads, dk):
    count = rows.shape[0]
    lead = before.shape[0]
    history = jnp.where(flag, 0.0, before.astype(F32))
    extended = jnp.concatenate([history, rows.astype(F32)], axis=0)
    mixed = extended[lead:] * taps[0:1]
    for lag in range(1, taps.shape[0]):
        mixed = mixed + pltpu.roll(extended, lag, 0)[lead:] * taps[lag : lag + 1]
    active = mixed * jax.nn.sigmoid(mixed)

    def stacked(part):
        return jnp.concatenate(
            [active[:, (3 * h + part) * dk : (3 * h + part + 1) * dk] for h in range(heads)], axis=0
        )

    query, key, value = stacked(0), stacked(1), stacked(2)
    query = query * (
        lax.rsqrt(jnp.sum(query * query, axis=-1, keepdims=True) + EPSILON) * dk ** (-0.5)
    )
    key = key * lax.rsqrt(jnp.sum(key * key, axis=-1, keepdims=True) + EPSILON)
    beta = jnp.concatenate([gating[:, h : h + 1] for h in range(heads)], axis=0)

    size = heads * count
    row = lax.broadcasted_iota(jnp.int32, (size, size), 0)
    col = lax.broadcasted_iota(jnp.int32, (size, size), 1)
    far = row ^ col
    same = (far < count) & (row >= col)
    keys = two(key)
    gram = mm3(keys, keys, mm_nt)
    lower = jnp.where(same & (row > col), beta * gram, 0.0)
    inverse = jnp.where(row == col, 1.0, 0.0) - jnp.where(far == 1, lower, 0.0)
    step = 2
    while step < count:
        corner = two(jnp.where((far >= step) & (far < 2 * step), lower, 0.0))
        halves = two(inverse)
        inverse = inverse - mm3(halves, two(mm3(corner, halves)))
        step *= 2
    target = jnp.concatenate([key * beta, value * beta], axis=1)
    solved = mm3(two(inverse), two(target)).astype(BF16)
    query16 = query.astype(BF16)
    scores = jnp.where(same, mm_nt(query16, keys[0]), 0.0).astype(BF16)
    mixed_in = mm(scores, solved)
    out_query = (query - mixed_in[:, :dk]).astype(BF16)
    out_base = mixed_in[:, dk:]
    moves = [
        mm_tn(keys[0][h * count : (h + 1) * count], solved[h * count : (h + 1) * count])
        for h in range(heads)
    ]
    return out_query, out_base, moves


def intra_kernel(per, heads, dk, flags, first_ref, before_ref, rows_ref, taps_ref, gate_ref,
                 query_ref, base_ref, decay_ref, add_ref):
    step = pl.program_id(0)
    taps = taps_ref[...]
    for j in range(per):
        if j == 0:
            before = jnp.where(step == 0, first_ref[...], before_ref[...])
        else:
            before = rows_ref[j * SPAN - 16 : j * SPAN]
        out_query, out_base, moves = intra_one(
            flags[step * per + j] > 0, before, rows_ref[j * SPAN : (j + 1) * SPAN], taps,
            gate_ref[j * SPAN : (j + 1) * SPAN], heads, dk,
        )
        query_ref[j] = out_query
        base_ref[j] = out_base
        for h in range(heads):
            decay_ref[j, h] = moves[h][:, :dk].astype(BF16)
            add_ref[j, h] = moves[h][:, dk:]


def intra(flags, first, projected, taps, gating, heads, dk, per=2):
    total, width = projected.shape
    spans = total // SPAN
    size = heads * SPAN
    grid = spans // per
    ahead = per * SPAN // 16
    return pl.pallas_call(
        partial(intra_kernel, per, heads, dk),
        grid_spec=pltpu.PrefetchScalarGridSpec(
            num_scalar_prefetch=1,
            grid=(grid,),
            in_specs=[
                pl.BlockSpec((16, width), lambda i, f: (0, 0)),
                pl.BlockSpec((16, width), lambda i, f: (jnp.maximum(i * ahead - 1, 0), 0)),
                pl.BlockSpec((per * SPAN, width), lambda i, f: (i, 0)),
                pl.BlockSpec(taps.shape, lambda i, f: (0, 0)),
                pl.BlockSpec((per * SPAN, heads), lambda i, f: (i, 0)),
            ],
            out_specs=[
                pl.BlockSpec((per, size, dk), lambda i, f: (i, 0, 0)),
                pl.BlockSpec((per, size, dk), lambda i, f: (i, 0, 0)),
                pl.BlockSpec((per, heads, dk, dk), lambda i, f: (i, 0, 0, 0)),
                pl.BlockSpec((per, heads, dk, dk), lambda i, f: (i, 0, 0, 0)),
            ],
        ),
        out_shape=[
            jax.ShapeDtypeStruct((spans, size, dk), BF16),
            jax.ShapeDtypeStruct((spans, size, dk), F32),
            jax.ShapeDtypeStruct((spans, heads, dk, dk), BF16),
            jax.ShapeDtypeStruct((spans, heads, dk, dk), F32),
        ],
        compiler_params=pltpu.CompilerParams(vmem_limit_bytes=40 * MIB),
        cost_estimate=pl.CostEstimate(
            flops=60_000_000_000, bytes_accessed=200_000_000, transcendentals=0
        ),
        name="intra",
    )(flags, first, projected, projected, taps, gating)


def tail_kernel(heads, start, decay_ref, add_ref, prior_ref, out_ref, memory):
    memory[...] = prior_ref[0]

    def body(i, carry):
        for h in range(heads):
            old = memory[h]
            memory[h] = old + add_ref[i, h] - mm(decay_ref[i, h], old.astype(BF16))
        return carry

    lax.fori_loop(start[0], decay_ref.shape[0], body, 0)
    out_ref[...] = memory[...].astype(BF16)


def tail(start, decay, add, prior):
    spans, heads, dk, _ = decay.shape
    slots = prior.shape[0]
    return pl.pallas_call(
        partial(tail_kernel, heads),
        grid_spec=pltpu.PrefetchScalarGridSpec(
            num_scalar_prefetch=1,
            grid=(1,),
            in_specs=[
                pl.BlockSpec(decay.shape, lambda i, s: (0, 0, 0, 0)),
                pl.BlockSpec(add.shape, lambda i, s: (0, 0, 0, 0)),
                pl.BlockSpec((1, heads, dk, dk), lambda i, s: (slots - 1, 0, 0, 0)),
            ],
            out_specs=pl.BlockSpec((heads, dk, dk), lambda i, s: (0, 0, 0)),
            scratch_shapes=[pltpu.VMEM((heads, dk, dk), F32)],
        ),
        out_shape=jax.ShapeDtypeStruct((heads, dk, dk), BF16),
        compiler_params=pltpu.CompilerParams(vmem_limit_bytes=40 * MIB),
        name="tail",
    )(start, decay, add, prior)


def scan_kernel(heads, dk, seg, starts, dest, linked, decay_ref, add_ref, query_ref, base_ref,
                prior_ref, handed_ref, gain_ref, out_ref, send_ref, memory):
    i = pl.program_id(0)

    @pl.when(starts[i] > 0)
    def _():
        memory[...] = prior_ref[0]

    @pl.when((i == 0) & (linked[0] > 0))
    def _():
        memory[...] = handed_ref[...].astype(F32)

    for h in range(heads):
        old = memory[h]
        old16 = old.astype(BF16)
        at = slice(h * SPAN, (h + 1) * SPAN)
        rows = mm(query_ref[0, at], old16) + base_ref[0, at]
        rows = rows * lax.rsqrt(jnp.mean(rows * rows, axis=-1, keepdims=True) + EPSILON)
        out_ref[:, h * dk : (h + 1) * dk] = (rows * gain_ref[...]).astype(BF16)
        new = old + add_ref[0, h] - mm(decay_ref[0, h], old16)
        memory[h] = new
        send_ref[0, h] = new.astype(BF16)


def scan(seg, starts, dest, linked, decay, add, query, base, prior, handed, gain, slots):
    spans, heads, dk, _ = decay.shape
    size = heads * SPAN
    return pl.pallas_call(
        partial(scan_kernel, heads, dk),
        grid_spec=pltpu.PrefetchScalarGridSpec(
            num_scalar_prefetch=4,
            grid=(spans,),
            in_specs=[
                pl.BlockSpec((1, heads, dk, dk), lambda i, g, s, d, k: (i, 0, 0, 0)),
                pl.BlockSpec((1, heads, dk, dk), lambda i, g, s, d, k: (i, 0, 0, 0)),
                pl.BlockSpec((1, size, dk), lambda i, g, s, d, k: (i, 0, 0)),
                pl.BlockSpec((1, size, dk), lambda i, g, s, d, k: (i, 0, 0)),
                pl.BlockSpec((1, heads, dk, dk), lambda i, g, s, d, k: (g[i], 0, 0, 0)),
                pl.BlockSpec((heads, dk, dk), lambda i, g, s, d, k: (0, 0, 0)),
                pl.BlockSpec((1, dk), lambda i, g, s, d, k: (0, 0)),
            ],
            out_specs=[
                pl.BlockSpec((SPAN, heads * dk), lambda i, g, s, d, k: (i, 0)),
                pl.BlockSpec((1, heads, dk, dk), lambda i, g, s, d, k: (d[i], 0, 0, 0)),
            ],
            scratch_shapes=[pltpu.VMEM((heads, dk, dk), F32)],
        ),
        out_shape=[
            jax.ShapeDtypeStruct((spans * SPAN, heads * dk), BF16),
            jax.ShapeDtypeStruct((slots, heads, dk, dk), BF16),
        ],
        compiler_params=pltpu.CompilerParams(vmem_limit_bytes=40 * MIB),
        cost_estimate=pl.CostEstimate(
            flops=10_000_000_000, bytes_accessed=40_000_000, transcendentals=0
        ),
        name="scan",
    )(seg, starts, dest, linked, decay, add, query, base, prior, handed, gain)


def place_kernel(index, x_ref, o_ref):
    o_ref[...] = x_ref[...].astype(F32)


def place(index, got, count):
    _, heads, dk, _ = got.shape
    return pl.pallas_call(
        place_kernel,
        grid_spec=pltpu.PrefetchScalarGridSpec(
            num_scalar_prefetch=1,
            grid=(count,),
            in_specs=[pl.BlockSpec((1, heads, dk, dk), lambda p, s: (s[p], 0, 0, 0))],
            out_specs=pl.BlockSpec((1, heads, dk, dk), lambda p, s: (p, 0, 0, 0)),
        ),
        out_shape=jax.ShapeDtypeStruct((count, heads, dk, dk), F32),
        name="place",
    )(index, got)


CAP = 2


def page_plan(page_table, requests):
    me = lax.axis_index("group")
    groups = lax.axis_size("group")
    tables = lax.all_gather(page_table, "group", axis=0, tiled=True).reshape(groups, requests)
    owner = tables // requests
    earlier = jnp.tril(jnp.ones((requests, requests), jnp.int32), -1)
    rank = jnp.sum((owner[:, :, None] == owner[:, None, :]) * earlier[None], axis=2)
    mine = jnp.arange(groups, dtype=jnp.int32) == me
    outgoing = jnp.sum(jnp.where(mine[:, None], owner * CAP + rank, 0), axis=0)
    wanted = me * requests + jnp.arange(requests, dtype=jnp.int32)
    sources = jnp.arange(groups, dtype=jnp.int32)[:, None] * CAP + rank
    hit = tables[:, :, None] == wanted[None, None, :]
    incoming = jnp.sum(jnp.where(hit, sources[:, :, None], 0), axis=(0, 1))
    return outgoing.astype(jnp.int32), incoming.astype(jnp.int32)


def shards(
    tokens,
    in_gain,
    trainer_qkv,
    head_order,
    conv_weight,
    beta_weight,
    beta_bias,
    out_gain,
    lengths,
    prior_states,
    page_table,
    o_weight,
    gate_weight,
    up_weight,
    down_weight,
):
    mp_count = lax.axis_size("mp")
    group_count = lax.axis_size("group")
    head_total = head_order.shape[0]
    local_heads = head_total // mp_count
    dk = prior_states.shape[2]
    requests = prior_states.shape[0]
    joined_width = 3 * dk
    gathered = lax.all_gather(tokens, "mp", axis=1, tiled=True)
    token_total = gathered.shape[0]
    spans = token_total // SPAN
    heads_of = jnp.arange(head_total, dtype=jnp.int32)
    slot_of_head = jnp.sum(
        jnp.where(head_order[None, :] == heads_of[:, None], heads_of[None, :], 0), axis=1
    ).astype(jnp.int32)
    ordered = order_heads(trainer_qkv, slot_of_head, mp_count, head_total, joined_width)
    shared = lax.all_to_all(ordered, "mp", split_axis=0, concat_axis=0)
    arranged = lax.all_gather(
        shared.reshape(-1, local_heads * joined_width), "group", axis=0, tiled=True
    )
    normed = normalize_rows(gathered, in_gain).astype(BF16)
    gating_all = jax.nn.sigmoid(
        jnp.dot(normed, beta_weight, preferred_element_type=F32) + beta_bias
    )
    projected = jnp.dot(normed, arranged, preferred_element_type=F32).astype(BF16)

    row = lengths[0].astype(jnp.int32)
    order = jnp.arange(requests, dtype=jnp.int32)
    starts = jnp.sum(jnp.where(order[None, :] < order[:, None], row[None, :], 0), axis=1)
    span_ids = jnp.arange(spans, dtype=jnp.int32)
    seg_of_span = jnp.sum((span_ids[:, None] >= starts[None, :]).astype(jnp.int32), axis=1) - 1
    is_start = jnp.any(span_ids[:, None] == starts[None, :], axis=1).astype(jnp.int32)
    linked = (lax.axis_index("group") > 0).astype(jnp.int32)
    begins = is_start * jnp.where(span_ids == 0, 1 - linked, 1)
    outgoing, incoming = page_plan(page_table, requests)
    dest = jnp.sum(
        jnp.where(seg_of_span[:, None] == order[None, :], outgoing[None, :], 0), axis=1
    ).astype(jnp.int32)

    behind = from_behind(projected[token_total - 16 :], "group", 1)
    query, base, decay, add = intra(
        begins, behind, projected, conv_weight, gating_all, local_heads, dk
    )
    last = tail(starts[-1:].astype(jnp.int32), decay, add, prior_states)
    handed = from_behind(last, "group", 1)
    attended, leaving = scan(
        seg_of_span.astype(jnp.int32), is_start, dest, linked[None], decay, add, query, base,
        prior_states, handed, out_gain[None], group_count * CAP,
    )
    arrived = lax.all_to_all(leaving, "group", split_axis=0, concat_axis=0, tiled=True)
    state_pages = place(incoming, arrived, requests)

    mixer_terms = jnp.dot(
        attended,
        lax.all_gather(o_weight, "group", axis=1, tiled=True),
        preferred_element_type=F32,
    ).astype(BF16)
    mixer_sum = lax.psum_scatter(mixer_terms, "mp", scatter_dimension=1, tiled=True).astype(F32)
    residual_one = (tokens.astype(F32) + mixer_sum).astype(BF16)
    mixed_rows = lax.all_gather(residual_one, "mp", axis=1, tiled=True)
    post_normed = normalize_rows(mixed_rows, 1.0).astype(BF16)
    gate_part = jnp.dot(
        post_normed,
        lax.all_gather(gate_weight, "group", axis=0, tiled=True),
        preferred_element_type=F32,
    )
    up_part = jnp.dot(
        post_normed,
        lax.all_gather(up_weight, "group", axis=0, tiled=True),
        preferred_element_type=F32,
    )
    hidden = (jax.nn.silu(gate_part) * up_part).astype(BF16)
    feed_terms = jnp.dot(
        hidden,
        lax.all_gather(down_weight, "group", axis=1, tiled=True),
        preferred_element_type=F32,
    ).astype(BF16)
    feed_sum = lax.psum_scatter(feed_terms, "mp", scatter_dimension=1, tiled=True).astype(F32)
    layer_out = (residual_one.astype(F32) + feed_sum).astype(BF16)
    return (attended, state_pages, layer_out)


def solution(mesh):
    in_specs = (
        P("group", "mp"),
        P(),
        P(("group", "mp"), None),
        P(),
        P(None, "mp"),
        P(None, "mp"),
        P("mp"),
        P(),
        P("group", None),
        P("group", "mp", None, None),
        P("group"),
        P("mp", "group"),
        P("group", "mp"),
        P("group", "mp"),
        P("mp", "group"),
    )
    out_specs = (P("group", "mp"), P("group", "mp", None, None), P("group", "mp"))
    return jax.shard_map(shards, mesh=mesh, in_specs=in_specs, out_specs=out_specs, check_vma=False)
```

```python
from functools import partial

import jax
import jax.numpy as jnp
from jax import lax
from jax.experimental import pallas as pl
from jax.experimental.pallas import tpu as pltpu
from jax.sharding import PartitionSpec as P

SPAN = 64
EPSILON = 1e-06
F32 = jnp.float32
BF16 = jnp.bfloat16
MIB = 1 << 20


def from_behind(value, axis, steps):
    count = lax.axis_size(axis)
    initial, last = (max(0, -steps), min(count, count - steps))
    return lax.ppermute(value, axis, [(source, source + steps) for source in range(initial, last)])


def swap(value, bit):
    return lax.ppermute(value, "mp", [(i, i ^ bit) for i in range(lax.axis_size("mp"))])


def share_columns(block):
    me = lax.axis_index("mp")
    held = [block]
    bit = lax.axis_size("mp") // 2
    while bit:
        low = (me & bit) == 0
        pairs = [(entry, swap(entry, bit)) for entry in held]
        held = [part for e, g in pairs for part in (jnp.where(low, e, g), jnp.where(low, g, e))]
        bit //= 2
    return jnp.concatenate(held, axis=1)


def product_shared(rows, weight):
    me = lax.axis_index("mp")
    count = lax.axis_size("mp")
    part = weight.shape[1] // count
    terms = {}
    for apart in range(count):
        piece = lax.dynamic_slice_in_dim(weight, (me ^ apart) * part, part, 1)
        terms[apart] = jnp.dot(rows, piece, preferred_element_type=F32)
    bit = 1
    while bit < count // 2:
        got = {r ^ bit: swap(terms[r].astype(BF16), bit) for r in sorted(terms, reverse=True) if r & bit}
        terms = {r: terms[r] + got[r].astype(F32) for r in sorted(got)}
        bit *= 2
    return terms[0], swap(terms[bit].astype(BF16), bit)


def normalize_rows(matrix, scaling):
    widened = matrix.astype(F32)
    return (
        widened * lax.rsqrt(jnp.mean(widened * widened, axis=-1, keepdims=True) + EPSILON) * scaling
    )


def mm(a, b):
    return lax.dot_general(a, b, (((1,), (0,)), ((), ())), preferred_element_type=F32)


def mm_nt(a, b):
    return lax.dot_general(a, b, (((1,), (1,)), ((), ())), preferred_element_type=F32)


def mm_tn(a, b):
    return lax.dot_general(a, b, (((0,), (0,)), ((), ())), preferred_element_type=F32)


def two(x):
    high = x.astype(BF16)
    return high, (x - high.astype(F32)).astype(BF16)


def mm3(a, b, product=mm):
    return product(a[0], b[0]) + (product(a[0], b[1]) + product(a[1], b[0]))


def order_kernel(slot_ref, x_ref, o_ref):
    o_ref[0] = x_ref[...].astype(BF16)


def order_heads(trainer, slot_of_head, parts, heads, joined):
    rows = trainer.shape[0]
    per = heads // parts
    return pl.pallas_call(
        order_kernel,
        grid_spec=pltpu.PrefetchScalarGridSpec(
            num_scalar_prefetch=1,
            grid=(heads,),
            in_specs=[pl.BlockSpec((rows, joined), lambda h, s: (0, s[h]))],
            out_specs=pl.BlockSpec((1, rows, joined), lambda h, s: (h // per, 0, h % per)),
        ),
        out_shape=jax.ShapeDtypeStruct((parts, rows, per * joined), BF16),
        name="order_heads",
    )(slot_of_head, trainer)


def intra_one(flag, before, rows, taps, gating, heads, dk):
    count = rows.shape[0]
    lead = before.shape[0]
    history = jnp.where(flag, 0.0, before.astype(F32))
    extended = jnp.concatenate([history, rows.astype(F32)], axis=0)
    mixed = extended[lead:] * taps[0:1]
    for lag in range(1, taps.shape[0]):
        mixed = mixed + pltpu.roll(extended, lag, 0)[lead:] * taps[lag : lag + 1]
    active = mixed * jax.nn.sigmoid(mixed)

    def stacked(part):
        return jnp.concatenate(
            [active[:, (3 * h + part) * dk : (3 * h + part + 1) * dk] for h in range(heads)], axis=0
        )

    query, key, value = stacked(0), stacked(1), stacked(2)
    query = query * (
        lax.rsqrt(jnp.sum(query * query, axis=-1, keepdims=True) + EPSILON) * dk ** (-0.5)
    )
    key = key * lax.rsqrt(jnp.sum(key * key, axis=-1, keepdims=True) + EPSILON)
    beta = jnp.concatenate([gating[:, h : h + 1] for h in range(heads)], axis=0)

    size = heads * count
    row = lax.broadcasted_iota(jnp.int32, (size, size), 0)
    col = lax.broadcasted_iota(jnp.int32, (size, size), 1)
    far = row ^ col
    same = (far < count) & (row >= col)
    keys = two(key)
    gram = mm3(keys, keys, mm_nt)
    lower = jnp.where(same & (row > col), beta * gram, 0.0)
    inverse = jnp.where(row == col, 1.0, 0.0) - jnp.where(far == 1, lower, 0.0)
    step = 2
    while step < count:
        corner = two(jnp.where((far >= step) & (far < 2 * step), lower, 0.0))
        halves = two(inverse)
        inverse = inverse - mm3(halves, two(mm3(corner, halves)))
        step *= 2
    target = jnp.concatenate([key * beta, value * beta], axis=1)
    solved = mm3(two(inverse), two(target)).astype(BF16)
    query16 = query.astype(BF16)
    scores = jnp.where(same, mm_nt(query16, keys[0]), 0.0).astype(BF16)
    mixed_in = mm(scores, solved)
    out_query = (query - mixed_in[:, :dk]).astype(BF16)
    out_base = mixed_in[:, dk:]
    moves = [
        mm_tn(keys[0][h * count : (h + 1) * count], solved[h * count : (h + 1) * count])
        for h in range(heads)
    ]
    return out_query, out_base, moves


def intra_kernel(per, heads, dk, flags, first_ref, before_ref, rows_ref, taps_ref, gate_ref,
                 query_ref, base_ref, decay_ref, add_ref):
    step = pl.program_id(0)
    taps = taps_ref[...]
    for j in range(per):
        if j == 0:
            before = jnp.where(step == 0, first_ref[...], before_ref[...])
        else:
            before = rows_ref[j * SPAN - 16 : j * SPAN]
        out_query, out_base, moves = intra_one(
            flags[step * per + j] > 0, before, rows_ref[j * SPAN : (j + 1) * SPAN], taps,
            gate_ref[j * SPAN : (j + 1) * SPAN], heads, dk,
        )
        query_ref[j] = out_query
        base_ref[j] = out_base
        for h in range(heads):
            decay_ref[j, h] = moves[h][:, :dk].astype(BF16)
            add_ref[j, h] = moves[h][:, dk:]


def intra(flags, first, projected, taps, gating, heads, dk, per=2):
    total, width = projected.shape
    spans = total // SPAN
    size = heads * SPAN
    grid = spans // per
    ahead = per * SPAN // 16
    return pl.pallas_call(
        partial(intra_kernel, per, heads, dk),
        grid_spec=pltpu.PrefetchScalarGridSpec(
            num_scalar_prefetch=1,
            grid=(grid,),
            in_specs=[
                pl.BlockSpec((16, width), lambda i, f: (0, 0)),
                pl.BlockSpec((16, width), lambda i, f: (jnp.maximum(i * ahead - 1, 0), 0)),
                pl.BlockSpec((per * SPAN, width), lambda i, f: (i, 0)),
                pl.BlockSpec(taps.shape, lambda i, f: (0, 0)),
                pl.BlockSpec((per * SPAN, heads), lambda i, f: (i, 0)),
            ],
            out_specs=[
                pl.BlockSpec((per, size, dk), lambda i, f: (i, 0, 0)),
                pl.BlockSpec((per, size, dk), lambda i, f: (i, 0, 0)),
                pl.BlockSpec((per, heads, dk, dk), lambda i, f: (i, 0, 0, 0)),
                pl.BlockSpec((per, heads, dk, dk), lambda i, f: (i, 0, 0, 0)),
            ],
        ),
        out_shape=[
            jax.ShapeDtypeStruct((spans, size, dk), BF16),
            jax.ShapeDtypeStruct((spans, size, dk), F32),
            jax.ShapeDtypeStruct((spans, heads, dk, dk), BF16),
            jax.ShapeDtypeStruct((spans, heads, dk, dk), F32),
        ],
        compiler_params=pltpu.CompilerParams(vmem_limit_bytes=40 * MIB),
        cost_estimate=pl.CostEstimate(
            flops=60_000_000_000, bytes_accessed=200_000_000, transcendentals=0
        ),
        name="intra",
    )(flags, first, projected, projected, taps, gating)


def tail_kernel(heads, start, decay_ref, add_ref, prior_ref, out_ref, memory):
    memory[...] = prior_ref[0]

    def body(i, carry):
        for h in range(heads):
            old = memory[h]
            memory[h] = old + add_ref[i, h] - mm(decay_ref[i, h], old.astype(BF16))
        return carry

    lax.fori_loop(start[0], decay_ref.shape[0], body, 0)
    out_ref[...] = memory[...].astype(BF16)


def tail(start, decay, add, prior):
    spans, heads, dk, _ = decay.shape
    slots = prior.shape[0]
    return pl.pallas_call(
        partial(tail_kernel, heads),
        grid_spec=pltpu.PrefetchScalarGridSpec(
            num_scalar_prefetch=1,
            grid=(1,),
            in_specs=[
                pl.BlockSpec(decay.shape, lambda i, s: (0, 0, 0, 0)),
                pl.BlockSpec(add.shape, lambda i, s: (0, 0, 0, 0)),
                pl.BlockSpec((1, heads, dk, dk), lambda i, s: (slots - 1, 0, 0, 0)),
            ],
            out_specs=pl.BlockSpec((heads, dk, dk), lambda i, s: (0, 0, 0)),
            scratch_shapes=[pltpu.VMEM((heads, dk, dk), F32)],
        ),
        out_shape=jax.ShapeDtypeStruct((heads, dk, dk), BF16),
        compiler_params=pltpu.CompilerParams(vmem_limit_bytes=40 * MIB),
        name="tail",
    )(start, decay, add, prior)


def scan_kernel(heads, dk, seg, starts, dest, linked, decay_ref, add_ref, query_ref, base_ref,
                prior_ref, handed_ref, gain_ref, out_ref, send_ref, memory):
    i = pl.program_id(0)

    @pl.when(starts[i] > 0)
    def _():
        memory[...] = prior_ref[0]

    @pl.when((i == 0) & (linked[0] > 0))
    def _():
        memory[...] = handed_ref[...].astype(F32)

    for h in range(heads):
        old = memory[h]
        old16 = old.astype(BF16)
        at = slice(h * SPAN, (h + 1) * SPAN)
        rows = mm(query_ref[0, at], old16) + base_ref[0, at]
        rows = rows * lax.rsqrt(jnp.mean(rows * rows, axis=-1, keepdims=True) + EPSILON)
        out_ref[:, h * dk : (h + 1) * dk] = (rows * gain_ref[...]).astype(BF16)
        new = old + add_ref[0, h] - mm(decay_ref[0, h], old16)
        memory[h] = new
        send_ref[0, h] = new.astype(BF16)


def scan(seg, starts, dest, linked, decay, add, query, base, prior, handed, gain, slots):
    spans, heads, dk, _ = decay.shape
    size = heads * SPAN
    return pl.pallas_call(
        partial(scan_kernel, heads, dk),
        grid_spec=pltpu.PrefetchScalarGridSpec(
            num_scalar_prefetch=4,
            grid=(spans,),
            in_specs=[
                pl.BlockSpec((1, heads, dk, dk), lambda i, g, s, d, k: (i, 0, 0, 0)),
                pl.BlockSpec((1, heads, dk, dk), lambda i, g, s, d, k: (i, 0, 0, 0)),
                pl.BlockSpec((1, size, dk), lambda i, g, s, d, k: (i, 0, 0)),
                pl.BlockSpec((1, size, dk), lambda i, g, s, d, k: (i, 0, 0)),
                pl.BlockSpec((1, heads, dk, dk), lambda i, g, s, d, k: (g[i], 0, 0, 0)),
                pl.BlockSpec((heads, dk, dk), lambda i, g, s, d, k: (0, 0, 0)),
                pl.BlockSpec((1, dk), lambda i, g, s, d, k: (0, 0)),
            ],
            out_specs=[
                pl.BlockSpec((SPAN, heads * dk), lambda i, g, s, d, k: (i, 0)),
                pl.BlockSpec((1, heads, dk, dk), lambda i, g, s, d, k: (d[i], 0, 0, 0)),
            ],
            scratch_shapes=[pltpu.VMEM((heads, dk, dk), F32)],
        ),
        out_shape=[
            jax.ShapeDtypeStruct((spans * SPAN, heads * dk), BF16),
            jax.ShapeDtypeStruct((slots, heads, dk, dk), BF16),
        ],
        compiler_params=pltpu.CompilerParams(vmem_limit_bytes=40 * MIB),
        cost_estimate=pl.CostEstimate(
            flops=10_000_000_000, bytes_accessed=40_000_000, transcendentals=0
        ),
        name="scan",
    )(seg, starts, dest, linked, decay, add, query, base, prior, handed, gain)


def place_kernel(index, x_ref, o_ref):
    o_ref[...] = x_ref[...].astype(F32)


def place(index, got, count):
    _, heads, dk, _ = got.shape
    return pl.pallas_call(
        place_kernel,
        grid_spec=pltpu.PrefetchScalarGridSpec(
            num_scalar_prefetch=1,
            grid=(count,),
            in_specs=[pl.BlockSpec((1, heads, dk, dk), lambda p, s: (s[p], 0, 0, 0))],
            out_specs=pl.BlockSpec((1, heads, dk, dk), lambda p, s: (p, 0, 0, 0)),
        ),
        out_shape=jax.ShapeDtypeStruct((count, heads, dk, dk), F32),
        name="place",
    )(index, got)


CAP = 2


def page_plan(page_table, requests):
    me = lax.axis_index("group")
    groups = lax.axis_size("group")
    tables = lax.all_gather(page_table, "group", axis=0, tiled=True).reshape(groups, requests)
    owner = tables // requests
    earlier = jnp.tril(jnp.ones((requests, requests), jnp.int32), -1)
    rank = jnp.sum((owner[:, :, None] == owner[:, None, :]) * earlier[None], axis=2)
    mine = jnp.arange(groups, dtype=jnp.int32) == me
    outgoing = jnp.sum(jnp.where(mine[:, None], owner * CAP + rank, 0), axis=0)
    wanted = me * requests + jnp.arange(requests, dtype=jnp.int32)
    sources = jnp.arange(groups, dtype=jnp.int32)[:, None] * CAP + rank
    hit = tables[:, :, None] == wanted[None, None, :]
    incoming = jnp.sum(jnp.where(hit, sources[:, :, None], 0), axis=(0, 1))
    return outgoing.astype(jnp.int32), incoming.astype(jnp.int32)


def shards(
    tokens,
    in_gain,
    trainer_qkv,
    head_order,
    conv_weight,
    beta_weight,
    beta_bias,
    out_gain,
    lengths,
    prior_states,
    page_table,
    o_weight,
    gate_weight,
    up_weight,
    down_weight,
):
    mp_count = lax.axis_size("mp")
    group_count = lax.axis_size("group")
    head_total = head_order.shape[0]
    local_heads = head_total // mp_count
    dk = prior_states.shape[2]
    requests = prior_states.shape[0]
    joined_width = 3 * dk
    gathered = share_columns(tokens)
    token_total = gathered.shape[0]
    spans = token_total // SPAN
    heads_of = jnp.arange(head_total, dtype=jnp.int32)
    slot_of_head = jnp.sum(
        jnp.where(head_order[None, :] == heads_of[:, None], heads_of[None, :], 0), axis=1
    ).astype(jnp.int32)
    ordered = order_heads(trainer_qkv, slot_of_head, mp_count, head_total, joined_width)
    shared = lax.all_to_all(ordered, "mp", split_axis=0, concat_axis=0)
    arranged = lax.all_gather(
        shared.reshape(-1, local_heads * joined_width), "group", axis=0, tiled=True
    )
    normed = normalize_rows(gathered, in_gain).astype(BF16)
    gating_all = jax.nn.sigmoid(
        jnp.dot(normed, beta_weight, preferred_element_type=F32) + beta_bias
    )
    projected = jnp.dot(normed, arranged, preferred_element_type=F32).astype(BF16)

    row = lengths[0].astype(jnp.int32)
    order = jnp.arange(requests, dtype=jnp.int32)
    starts = jnp.sum(jnp.where(order[None, :] < order[:, None], row[None, :], 0), axis=1)
    span_ids = jnp.arange(spans, dtype=jnp.int32)
    seg_of_span = jnp.sum((span_ids[:, None] >= starts[None, :]).astype(jnp.int32), axis=1) - 1
    is_start = jnp.any(span_ids[:, None] == starts[None, :], axis=1).astype(jnp.int32)
    linked = (lax.axis_index("group") > 0).astype(jnp.int32)
    begins = is_start * jnp.where(span_ids == 0, 1 - linked, 1)
    outgoing, incoming = page_plan(page_table, requests)
    dest = jnp.sum(
        jnp.where(seg_of_span[:, None] == order[None, :], outgoing[None, :], 0), axis=1
    ).astype(jnp.int32)

    behind = from_behind(projected[token_total - 16 :], "group", 1)
    query, base, decay, add = intra(
        begins, behind, projected, conv_weight, gating_all, local_heads, dk
    )
    o_full = lax.all_gather(o_weight, "group", axis=1, tiled=True)
    gate_full = lax.all_gather(gate_weight, "group", axis=0, tiled=True)
    up_full = lax.all_gather(up_weight, "group", axis=0, tiled=True)
    down_full = lax.all_gather(down_weight, "group", axis=1, tiled=True)
    decay, o_full = lax.optimization_barrier((decay, o_full))
    last = tail(starts[-1:].astype(jnp.int32), decay, add, prior_states)
    handed = from_behind(last, "group", 1)
    attended, leaving = scan(
        seg_of_span.astype(jnp.int32), is_start, dest, linked[None], decay, add, query, base,
        prior_states, handed, out_gain[None], group_count * CAP,
    )
    arrived = lax.all_to_all(leaving, "group", split_axis=0, concat_axis=0, tiled=True)
    kept, got = product_shared(attended, o_full)
    got, gate_full = lax.optimization_barrier((got, gate_full))
    residual_one = (tokens.astype(F32) + (kept + got.astype(F32))).astype(BF16)
    mixed_rows = share_columns(residual_one)
    post_normed = normalize_rows(mixed_rows, 1.0).astype(BF16)
    gate_part = jnp.dot(post_normed, gate_full, preferred_element_type=F32)
    up_part = jnp.dot(post_normed, up_full, preferred_element_type=F32)
    hidden = (jax.nn.silu(gate_part) * up_part).astype(BF16)
    hidden, arrived = lax.optimization_barrier((hidden, arrived))
    state_pages = place(incoming, arrived, requests)
    kept, got = product_shared(hidden, down_full)
    layer_out = (residual_one.astype(F32) + (kept + got.astype(F32))).astype(BF16)
    return (attended, state_pages, layer_out)


def solution(mesh):
    in_specs = (
        P("group", "mp"),
        P(),
        P(("group", "mp"), None),
        P(),
        P(None, "mp"),
        P(None, "mp"),
        P("mp"),
        P(),
        P("group", None),
        P("group", "mp", None, None),
        P("group"),
        P("mp", "group"),
        P("group", "mp"),
        P("group", "mp"),
        P("mp", "group"),
    )
    out_specs = (P("group", "mp"), P("group", "mp", None, None), P("group", "mp"))
    return jax.shard_map(shards, mesh=mesh, in_specs=in_specs, out_specs=out_specs, check_vma=False)
```

```python
from functools import partial

import jax
import jax.numpy as jnp
from jax import lax
from jax.experimental import pallas as pl
from jax.experimental.pallas import tpu as pltpu
from jax.sharding import PartitionSpec as P

SPAN = 64
EPSILON = 1e-06
F32 = jnp.float32
BF16 = jnp.bfloat16
MIB = 1 << 20


def from_behind(value, axis, steps):
    count = lax.axis_size(axis)
    initial, last = (max(0, -steps), min(count, count - steps))
    return lax.ppermute(value, axis, [(source, source + steps) for source in range(initial, last)])


def swap(value, bit):
    return lax.ppermute(value, "mp", [(i, i ^ bit) for i in range(lax.axis_size("mp"))])


def share_columns(block):
    me = lax.axis_index("mp")
    held = [block]
    bit = lax.axis_size("mp") // 2
    while bit:
        low = (me & bit) == 0
        pairs = [(entry, swap(entry, bit)) for entry in held]
        held = [part for e, g in pairs for part in (jnp.where(low, e, g), jnp.where(low, g, e))]
        bit //= 2
    return jnp.concatenate(held, axis=1)


def product_shared(rows, weight):
    me = lax.axis_index("mp")
    count = lax.axis_size("mp")
    part = weight.shape[1] // count
    terms = {}
    for apart in range(count):
        piece = lax.dynamic_slice_in_dim(weight, (me ^ apart) * part, part, 1)
        terms[apart] = jnp.dot(rows, piece, preferred_element_type=F32)
    bit = 1
    while bit < count // 2:
        got = {r ^ bit: swap(terms[r].astype(BF16), bit) for r in sorted(terms, reverse=True) if r & bit}
        terms = {r: terms[r] + got[r].astype(F32) for r in sorted(got)}
        bit *= 2
    return terms[0], swap(terms[bit].astype(BF16), bit)


def normalize_rows(matrix, scaling):
    widened = matrix.astype(F32)
    return (
        widened * lax.rsqrt(jnp.mean(widened * widened, axis=-1, keepdims=True) + EPSILON) * scaling
    )


def mm(a, b):
    return lax.dot_general(a, b, (((1,), (0,)), ((), ())), preferred_element_type=F32)


def mm_nt(a, b):
    return lax.dot_general(a, b, (((1,), (1,)), ((), ())), preferred_element_type=F32)


def mm_tn(a, b):
    return lax.dot_general(a, b, (((0,), (0,)), ((), ())), preferred_element_type=F32)


def two(x):
    high = x.astype(BF16)
    return high, (x - high.astype(F32)).astype(BF16)


def mm3(a, b, product=mm):
    return product(a[0], b[0]) + (product(a[0], b[1]) + product(a[1], b[0]))


def order_kernel(slot_ref, x_ref, o_ref):
    o_ref[0] = x_ref[...].astype(BF16)


def order_heads(trainer, slot_of_head, parts, heads, joined):
    rows = trainer.shape[0]
    per = heads // parts
    return pl.pallas_call(
        order_kernel,
        grid_spec=pltpu.PrefetchScalarGridSpec(
            num_scalar_prefetch=1,
            grid=(heads,),
            in_specs=[pl.BlockSpec((rows, joined), lambda h, s: (0, s[h]))],
            out_specs=pl.BlockSpec((1, rows, joined), lambda h, s: (h // per, 0, h % per)),
        ),
        out_shape=jax.ShapeDtypeStruct((parts, rows, per * joined), BF16),
        name="order_heads",
    )(slot_of_head, trainer)


def intra_one(flag, before, rows, taps, gating, heads, dk):
    count = rows.shape[0]
    lead = before.shape[0]
    history = jnp.where(flag, 0.0, before.astype(F32))
    extended = jnp.concatenate([history, rows.astype(F32)], axis=0)
    mixed = extended[lead:] * taps[0:1]
    for lag in range(1, taps.shape[0]):
        mixed = mixed + pltpu.roll(extended, lag, 0)[lead:] * taps[lag : lag + 1]
    active = mixed * jax.nn.sigmoid(mixed)

    def stacked(part):
        return jnp.concatenate(
            [active[:, (3 * h + part) * dk : (3 * h + part + 1) * dk] for h in range(heads)], axis=0
        )

    query, key, value = stacked(0), stacked(1), stacked(2)
    query = query * (
        lax.rsqrt(jnp.sum(query * query, axis=-1, keepdims=True) + EPSILON) * dk ** (-0.5)
    )
    key = key * lax.rsqrt(jnp.sum(key * key, axis=-1, keepdims=True) + EPSILON)
    beta = jnp.concatenate([gating[:, h : h + 1] for h in range(heads)], axis=0)

    size = heads * count
    row = lax.broadcasted_iota(jnp.int32, (size, size), 0)
    col = lax.broadcasted_iota(jnp.int32, (size, size), 1)
    far = row ^ col
    same = (far < count) & (row >= col)
    keys = two(key)
    gram = mm3(keys, keys, mm_nt)
    lower = jnp.where(same & (row > col), beta * gram, 0.0)
    inverse = jnp.where(row == col, 1.0, 0.0) - jnp.where(far == 1, lower, 0.0)
    step = 2
    while step < count:
        corner = two(jnp.where((far >= step) & (far < 2 * step), lower, 0.0))
        halves = two(inverse)
        inverse = inverse - mm3(halves, two(mm3(corner, halves)))
        step *= 2
    target = jnp.concatenate([key * beta, value * beta], axis=1)
    solved = mm3(two(inverse), two(target)).astype(BF16)
    query16 = query.astype(BF16)
    scores = jnp.where(same, mm_nt(query16, keys[0]), 0.0).astype(BF16)
    mixed_in = mm(scores, solved)
    out_query = (query - mixed_in[:, :dk]).astype(BF16)
    out_base = mixed_in[:, dk:]
    moves = [
        mm_tn(keys[0][h * count : (h + 1) * count], solved[h * count : (h + 1) * count])
        for h in range(heads)
    ]
    return out_query, out_base, moves


def intra_kernel(per, heads, dk, flags, first_ref, before_ref, rows_ref, taps_ref, gate_ref,
                 query_ref, base_ref, decay_ref, add_ref):
    step = pl.program_id(0)
    taps = taps_ref[...]
    for j in range(per):
        if j == 0:
            before = jnp.where(step == 0, first_ref[...], before_ref[...])
        else:
            before = rows_ref[j * SPAN - 16 : j * SPAN]
        out_query, out_base, moves = intra_one(
            flags[step * per + j] > 0, before, rows_ref[j * SPAN : (j + 1) * SPAN], taps,
            gate_ref[j * SPAN : (j + 1) * SPAN], heads, dk,
        )
        query_ref[j] = out_query
        base_ref[j] = out_base
        for h in range(heads):
            decay_ref[j, h] = moves[h][:, :dk].astype(BF16)
            add_ref[j, h] = moves[h][:, dk:]


def intra(flags, first, projected, taps, gating, heads, dk, per=2):
    total, width = projected.shape
    spans = total // SPAN
    size = heads * SPAN
    grid = spans // per
    ahead = per * SPAN // 16
    return pl.pallas_call(
        partial(intra_kernel, per, heads, dk),
        grid_spec=pltpu.PrefetchScalarGridSpec(
            num_scalar_prefetch=1,
            grid=(grid,),
            in_specs=[
                pl.BlockSpec((16, width), lambda i, f: (0, 0)),
                pl.BlockSpec((16, width), lambda i, f: (jnp.maximum(i * ahead - 1, 0), 0)),
                pl.BlockSpec((per * SPAN, width), lambda i, f: (i, 0)),
                pl.BlockSpec(taps.shape, lambda i, f: (0, 0)),
                pl.BlockSpec((per * SPAN, heads), lambda i, f: (i, 0)),
            ],
            out_specs=[
                pl.BlockSpec((per, size, dk), lambda i, f: (i, 0, 0)),
                pl.BlockSpec((per, size, dk), lambda i, f: (i, 0, 0)),
                pl.BlockSpec((per, heads, dk, dk), lambda i, f: (i, 0, 0, 0)),
                pl.BlockSpec((per, heads, dk, dk), lambda i, f: (i, 0, 0, 0)),
            ],
        ),
        out_shape=[
            jax.ShapeDtypeStruct((spans, size, dk), BF16),
            jax.ShapeDtypeStruct((spans, size, dk), F32),
            jax.ShapeDtypeStruct((spans, heads, dk, dk), BF16),
            jax.ShapeDtypeStruct((spans, heads, dk, dk), F32),
        ],
        compiler_params=pltpu.CompilerParams(vmem_limit_bytes=40 * MIB),
        cost_estimate=pl.CostEstimate(
            flops=60_000_000_000, bytes_accessed=200_000_000, transcendentals=0
        ),
        name="intra",
    )(flags, first, projected, projected, taps, gating)


def tail_kernel(heads, start, decay_ref, add_ref, prior_ref, out_ref, memory):
    memory[...] = prior_ref[0]

    def body(i, carry):
        for h in range(heads):
            old = memory[h]
            memory[h] = old + add_ref[i, h] - mm(decay_ref[i, h], old.astype(BF16))
        return carry

    lax.fori_loop(start[0], decay_ref.shape[0], body, 0)
    out_ref[...] = memory[...].astype(BF16)


def tail(start, decay, add, prior):
    spans, heads, dk, _ = decay.shape
    slots = prior.shape[0]
    return pl.pallas_call(
        partial(tail_kernel, heads),
        grid_spec=pltpu.PrefetchScalarGridSpec(
            num_scalar_prefetch=1,
            grid=(1,),
            in_specs=[
                pl.BlockSpec(decay.shape, lambda i, s: (0, 0, 0, 0)),
                pl.BlockSpec(add.shape, lambda i, s: (0, 0, 0, 0)),
                pl.BlockSpec((1, heads, dk, dk), lambda i, s: (slots - 1, 0, 0, 0)),
            ],
            out_specs=pl.BlockSpec((heads, dk, dk), lambda i, s: (0, 0, 0)),
            scratch_shapes=[pltpu.VMEM((heads, dk, dk), F32)],
        ),
        out_shape=jax.ShapeDtypeStruct((heads, dk, dk), BF16),
        compiler_params=pltpu.CompilerParams(vmem_limit_bytes=40 * MIB),
        name="tail",
    )(start, decay, add, prior)


def scan_kernel(heads, dk, seg, starts, dest, linked, decay_ref, add_ref, query_ref, base_ref,
                prior_ref, handed_ref, gain_ref, out_ref, send_ref, memory):
    i = pl.program_id(0)

    @pl.when(starts[i] > 0)
    def _():
        memory[...] = prior_ref[0]

    @pl.when((i == 0) & (linked[0] > 0))
    def _():
        memory[...] = handed_ref[...].astype(F32)

    for h in range(heads):
        old = memory[h]
        old16 = old.astype(BF16)
        at = slice(h * SPAN, (h + 1) * SPAN)
        rows = mm(query_ref[0, at], old16) + base_ref[0, at]
        rows = rows * lax.rsqrt(jnp.mean(rows * rows, axis=-1, keepdims=True) + EPSILON)
        out_ref[:, h * dk : (h + 1) * dk] = (rows * gain_ref[...]).astype(BF16)
        new = old + add_ref[0, h] - mm(decay_ref[0, h], old16)
        memory[h] = new
        send_ref[0, h] = new.astype(BF16)


def scan(seg, starts, dest, linked, decay, add, query, base, prior, handed, gain, slots):
    spans, heads, dk, _ = decay.shape
    size = heads * SPAN
    return pl.pallas_call(
        partial(scan_kernel, heads, dk),
        grid_spec=pltpu.PrefetchScalarGridSpec(
            num_scalar_prefetch=4,
            grid=(spans,),
            in_specs=[
                pl.BlockSpec((1, heads, dk, dk), lambda i, g, s, d, k: (i, 0, 0, 0)),
                pl.BlockSpec((1, heads, dk, dk), lambda i, g, s, d, k: (i, 0, 0, 0)),
                pl.BlockSpec((1, size, dk), lambda i, g, s, d, k: (i, 0, 0)),
                pl.BlockSpec((1, size, dk), lambda i, g, s, d, k: (i, 0, 0)),
                pl.BlockSpec((1, heads, dk, dk), lambda i, g, s, d, k: (g[i], 0, 0, 0)),
                pl.BlockSpec((heads, dk, dk), lambda i, g, s, d, k: (0, 0, 0)),
                pl.BlockSpec((1, dk), lambda i, g, s, d, k: (0, 0)),
            ],
            out_specs=[
                pl.BlockSpec((SPAN, heads * dk), lambda i, g, s, d, k: (i, 0)),
                pl.BlockSpec((1, heads, dk, dk), lambda i, g, s, d, k: (d[i], 0, 0, 0)),
            ],
            scratch_shapes=[pltpu.VMEM((heads, dk, dk), F32)],
        ),
        out_shape=[
            jax.ShapeDtypeStruct((spans * SPAN, heads * dk), BF16),
            jax.ShapeDtypeStruct((slots, heads, dk, dk), BF16),
        ],
        compiler_params=pltpu.CompilerParams(vmem_limit_bytes=40 * MIB),
        cost_estimate=pl.CostEstimate(
            flops=10_000_000_000, bytes_accessed=40_000_000, transcendentals=0
        ),
        name="scan",
    )(seg, starts, dest, linked, decay, add, query, base, prior, handed, gain)


def place_kernel(index, x_ref, o_ref):
    o_ref[...] = x_ref[...].astype(F32)


def place(index, got, count):
    _, heads, dk, _ = got.shape
    return pl.pallas_call(
        place_kernel,
        grid_spec=pltpu.PrefetchScalarGridSpec(
            num_scalar_prefetch=1,
            grid=(count,),
            in_specs=[pl.BlockSpec((1, heads, dk, dk), lambda p, s: (s[p], 0, 0, 0))],
            out_specs=pl.BlockSpec((1, heads, dk, dk), lambda p, s: (p, 0, 0, 0)),
        ),
        out_shape=jax.ShapeDtypeStruct((count, heads, dk, dk), F32),
        name="place",
    )(index, got)


CAP = 2


def page_plan(page_table, requests):
    me = lax.axis_index("group")
    groups = lax.axis_size("group")
    tables = lax.all_gather(page_table, "group", axis=0, tiled=True).reshape(groups, requests)
    owner = tables // requests
    earlier = jnp.tril(jnp.ones((requests, requests), jnp.int32), -1)
    rank = jnp.sum((owner[:, :, None] == owner[:, None, :]) * earlier[None], axis=2)
    mine = jnp.arange(groups, dtype=jnp.int32) == me
    outgoing = jnp.sum(jnp.where(mine[:, None], owner * CAP + rank, 0), axis=0)
    wanted = me * requests + jnp.arange(requests, dtype=jnp.int32)
    sources = jnp.arange(groups, dtype=jnp.int32)[:, None] * CAP + rank
    hit = tables[:, :, None] == wanted[None, None, :]
    incoming = jnp.sum(jnp.where(hit, sources[:, :, None], 0), axis=(0, 1))
    return outgoing.astype(jnp.int32), incoming.astype(jnp.int32)


def shards(
    tokens,
    in_gain,
    trainer_qkv,
    head_order,
    conv_weight,
    beta_weight,
    beta_bias,
    out_gain,
    lengths,
    prior_states,
    page_table,
    o_weight,
    gate_weight,
    up_weight,
    down_weight,
):
    mp_count = lax.axis_size("mp")
    group_count = lax.axis_size("group")
    head_total = head_order.shape[0]
    local_heads = head_total // mp_count
    dk = prior_states.shape[2]
    requests = prior_states.shape[0]
    joined_width = 3 * dk
    gathered = share_columns(tokens)
    token_total = gathered.shape[0]
    spans = token_total // SPAN
    heads_of = jnp.arange(head_total, dtype=jnp.int32)
    slot_of_head = jnp.sum(
        jnp.where(head_order[None, :] == heads_of[:, None], heads_of[None, :], 0), axis=1
    ).astype(jnp.int32)
    ordered = order_heads(trainer_qkv, slot_of_head, mp_count, head_total, joined_width)
    shared = lax.all_to_all(ordered, "mp", split_axis=0, concat_axis=0)
    arranged = lax.all_gather(
        shared.reshape(-1, local_heads * joined_width), "group", axis=0, tiled=True
    )
    normed = normalize_rows(gathered, in_gain).astype(BF16)
    gating_all = jax.nn.sigmoid(
        jnp.dot(normed, beta_weight, preferred_element_type=F32) + beta_bias
    )
    projected = jnp.dot(normed, arranged, preferred_element_type=F32).astype(BF16)

    row = lengths[0].astype(jnp.int32)
    order = jnp.arange(requests, dtype=jnp.int32)
    starts = jnp.sum(jnp.where(order[None, :] < order[:, None], row[None, :], 0), axis=1)
    span_ids = jnp.arange(spans, dtype=jnp.int32)
    seg_of_span = jnp.sum((span_ids[:, None] >= starts[None, :]).astype(jnp.int32), axis=1) - 1
    is_start = jnp.any(span_ids[:, None] == starts[None, :], axis=1).astype(jnp.int32)
    linked = (lax.axis_index("group") > 0).astype(jnp.int32)
    begins = is_start * jnp.where(span_ids == 0, 1 - linked, 1)
    outgoing, incoming = page_plan(page_table, requests)
    dest = jnp.sum(
        jnp.where(seg_of_span[:, None] == order[None, :], outgoing[None, :], 0), axis=1
    ).astype(jnp.int32)

    behind = from_behind(projected[token_total - 16 :], "group", 1)
    query, base, decay, add = intra(
        begins, behind, projected, conv_weight, gating_all, local_heads, dk
    )
    o_full = lax.all_gather(o_weight, "group", axis=0)
    gate_full = lax.all_gather(gate_weight, "group", axis=0, tiled=True)
    up_full = lax.all_gather(up_weight, "group", axis=0, tiled=True)
    down_full = lax.all_gather(down_weight, "group", axis=1, tiled=True)
    decay, o_full = lax.optimization_barrier((decay, o_full))
    last = tail(starts[-1:].astype(jnp.int32), decay, add, prior_states)
    handed = from_behind(last, "group", 1)
    attended, leaving = scan(
        seg_of_span.astype(jnp.int32), is_start, dest, linked[None], decay, add, query, base,
        prior_states, handed, out_gain[None], group_count * CAP,
    )
    arrived = lax.all_to_all(leaving, "group", split_axis=0, concat_axis=0, tiled=True)
    o_full = o_full.transpose(1, 0, 2).reshape(o_weight.shape[0], -1)
    kept, got = product_shared(attended, o_full)
    got, gate_full = lax.optimization_barrier((got, gate_full))
    residual_one = (tokens.astype(F32) + (kept + got.astype(F32))).astype(BF16)
    mixed_rows = share_columns(residual_one)
    post_normed = normalize_rows(mixed_rows, 1.0).astype(BF16)
    gate_part = jnp.dot(post_normed, gate_full, preferred_element_type=F32)
    up_part = jnp.dot(post_normed, up_full, preferred_element_type=F32)
    hidden = (jax.nn.silu(gate_part) * up_part).astype(BF16)
    hidden, arrived = lax.optimization_barrier((hidden, arrived))
    state_pages = place(incoming, arrived, requests)
    kept, got = product_shared(hidden, down_full)
    layer_out = (residual_one.astype(F32) + (kept + got.astype(F32))).astype(BF16)
    return (attended, state_pages, layer_out)


def solution(mesh):
    in_specs = (
        P("group", "mp"),
        P(),
        P(("group", "mp"), None),
        P(),
        P(None, "mp"),
        P(None, "mp"),
        P("mp"),
        P(),
        P("group", None),
        P("group", "mp", None, None),
        P("group"),
        P("mp", "group"),
        P("group", "mp"),
        P("group", "mp"),
        P("mp", "group"),
    )
    out_specs = (P("group", "mp"), P("group", "mp", None, None), P("group", "mp"))
    return jax.shard_map(shards, mesh=mesh, in_specs=in_specs, out_specs=out_specs, check_vma=False)
```
